512 devices in a mesh: lon: 32 (over z_hi, x, core), lat: 16 (over y, z_lo).
Axes of the slice: x: 4, y: 8, z: 8 (z_hi: 4, z_lo: 2; z = z_hi * 2 + z_lo), core: 2. Of those that a mesh axis runs over, the one named last changes fastest.
Arguments:
- field: bfloat16 [256, 256, 4096], P(None, 'lat', 'lon'), may hold values from -6 to 6
- cotangent: bfloat16 [256, 256, 4096], P(None, 'lat', 'lon'), may hold values from -6 to 6
- filters: bfloat16 [3, 256, 3, 17], P(None, 'lat'), may hold values from -1.5 to 1.5
- reach: int32 [256, 2], P('lat'), may hold values from -8 to 8, as said below
- mixing: bfloat16 [256, 3, 256], replicated, may hold values from -0.21875 to 0.21875
- bias: float32 [256], replicated, may hold values from -3 to 3
Outputs:
- out_field: bfloat16 [256, 256, 4096], P(None, 'lat', 'lon')
- grad_field: bfloat16 [256, 256, 4096], P(None, 'lat', 'lon')
- grad_mixing: float32 [256, 3, 256], P('lon')
The draws below stay inside these ranges and needn't reach their ends.
Inputs may be any that keep to these rules, and one draw needn't show every extreme that they name: Row i's filter support in longitude runs from offset reach[i, 0] to reach[i, 1]; it always holds offsets -1, 0 and 1, and the first and last rows of the grid span -8 to 8.
All inputs are finite; a program needn't handle non-finite values.
Results may differ from the reference program's by a relative error of at most 0.0056.
Values may be sent and summed in bfloat16 or wider, within the bound.
No kernel may reach another device: no remote copies, remote signals or barrier semaphores. Data moves between devices by JAX's collectives and lax.ppermute only.
A program may use at most 64 MiB of HBM per device.

```python
import math
import jax
import jax.numpy as jnp
from jax import lax

C = 256
K = 3
SMAX = 8
LAT_DEV = 16
NLAT = 256
NLON = 4096


def draw_reach(key, part):
    key = jax.random.fold_in(key, 11)
    first_key, second_key = jax.random.split(key)
    rows = jnp.arange(NLAT, dtype=jnp.int32)
    polar = jnp.minimum(rows, NLAT - 1 - rows)
    base = jnp.minimum(SMAX, 1 + NLAT // (3 * (polar + 1)))
    base = jnp.where(polar == 0, SMAX, base)
    low = -jnp.minimum(SMAX, base + jax.random.randint(first_key, (NLAT,), 0, 3))
    high = jnp.minimum(SMAX, base + jax.random.randint(second_key, (NLAT,), 0, 3))
    return jnp.stack([low, high], axis=1).astype(jnp.int32)


def with_spikes(drawn, key, source, target, parts, factor):
    def block_of(axis_at):
        return (jnp.arange(drawn.shape[axis_at]) // (drawn.shape[axis_at] // parts)).reshape((-1,) + (1,) * (drawn.ndim - 1 - axis_at))

    one_side = jax.random.permutation(key, parts)[block_of(target)]
    far = (block_of(target) + parts // 2) % parts
    return jnp.where((block_of(source) == one_side) | (block_of(source) == far), factor * drawn, drawn)


def level_of(rng, extent, shards, low, top_value):
    factor_of = 1.0
    for position, blocks in shards:
        heights = jax.random.uniform(jax.random.fold_in(jax.random.fold_in(rng, 6), position), (blocks,), jnp.float32, low / len(shards), top_value / len(shards))
        factor_of = factor_of * jnp.repeat(jnp.exp(heights), extent[position] // blocks).reshape((-1,) + (1,) * (len(extent) - 1 - position))
    return factor_of


def bell_draw(stream_key, extent, scale, most, shards=(), kind=jnp.bfloat16):
    loudness = level_of(stream_key, extent, shards, -0.22, 0.18) if shards else 1.0
    values = jax.random.normal(stream_key, extent, jnp.float32) * scale * loudness
    return jnp.minimum(jnp.maximum(values, -most), most).astype(kind)


def gaussian_with(rng, shape, deviation, limit, cuts, heavy, kind=jnp.bfloat16):
    result = deviation * jax.random.normal(rng, shape, jnp.float32)
    if cuts:
        result = result * level_of(rng, shape, cuts, -0.22, 0.18)
    return jnp.clip(with_spikes(result, jax.random.fold_in(rng, 3), *heavy), -limit, limit).astype(kind)


def setup_inputs(seed: int = 0) -> dict:
    arg_keys = jax.random.split(jax.random.key(seed), 7)
    field = bell_draw(arg_keys[0], (C, NLAT, NLON), 1.0, 6.0, ((1, 16), (2, 32)))
    cotangent = gaussian_with(arg_keys[1], (C, NLAT, NLON), 1.0, 6.0, ((1, 16), (2, 32)), (2, 0, 32, 2.75))
    filters = bell_draw(arg_keys[2], (K, NLAT, 3, 2 * SMAX + 1), 0.25, 1.5, ((1, 16),))
    reach = draw_reach(jax.random.fold_in(arg_keys[6], 71), 0)
    mixing = bell_draw(arg_keys[4], (C, K, C), (K * C) ** -0.5, 0.21875)
    bias = bell_draw(arg_keys[5], (C,), 0.5, 3.0, (), jnp.float32)
    return dict(field=field, cotangent=cotangent, filters=filters, reach=reach, mixing=mixing, bias=bias)


def gelu_pair(pre):
    root = 0.7978845608028654
    inner = root * (pre + 0.044715 * pre * pre * pre)
    tanh_v = jnp.tanh(inner)
    value = 0.5 * pre * (1.0 + tanh_v)
    slope = 0.5 * (1.0 + tanh_v) + 0.5 * pre * (1.0 - tanh_v * tanh_v) * root * (1.0 + 3.0 * 0.044715 * pre * pre)
    return (value, slope)

def wrap_lon(array):
    return jnp.concatenate([array[..., -SMAX:], array, array[..., :SMAX]], axis=-1)

def reference(field, cotangent, filters, reach, mixing, bias):
    taps = 2 * SMAX + 1
    offsets = jnp.arange(taps, dtype=jnp.int32) - SMAX
    inside = (reach[:, 0:1] <= offsets[None, :]) & (offsets[None, :] <= reach[:, 1:2])
    coef = filters * inside[None, :, None, :].astype(jnp.bfloat16)
    coef32 = coef.astype(jnp.float32)
    padded = jnp.pad(wrap_lon(field), ((0, 0), (1, 1), (0, 0)))
    coef_pad = jnp.pad(coef32, ((0, 0), (1, 1), (0, 0), (0, 0)))
    weights = mixing.astype(jnp.float32)
    blocks = NLAT // LAT_DEV

    def forward(total, index):
        start = (index * LAT_DEV).astype(jnp.int32)
        window = lax.dynamic_slice_in_dim(padded, start, LAT_DEV + 2, 1).astype(jnp.float32)
        rows_coef = lax.dynamic_slice_in_dim(coef32, start, LAT_DEV, 1)
        acc = jnp.zeros((K, C, LAT_DEV, NLON), jnp.float32)
        for r in range(3):
            for t in range(taps):
                acc = acc + rows_coef[:, None, :, r, t, None] * window[None, :, r:r + LAT_DEV, t:t + NLON]
        basis = lax.optimization_barrier(acc.astype(jnp.bfloat16)).astype(jnp.float32)
        pre = jnp.einsum('okc,kclq->olq', weights, basis) + bias[:, None, None].astype(jnp.float32)
        value, slope = gelu_pair(pre)
        local = lax.dynamic_slice_in_dim(field, start, LAT_DEV, 1).astype(jnp.float32)
        cot = lax.dynamic_slice_in_dim(cotangent, start, LAT_DEV, 1).astype(jnp.float32)
        out = (local + value).astype(jnp.bfloat16)
        grad_pre = lax.optimization_barrier((cot * slope).astype(jnp.bfloat16))
        total = total + jnp.einsum('olq,kclq->okc', grad_pre.astype(jnp.float32), basis)
        return (total, (out, grad_pre))
    start_total = jnp.zeros((C, K, C), jnp.float32)
    grad_sum, (outs, pres) = lax.scan(forward, start_total, jnp.arange(blocks, dtype=jnp.int32))
    out_field = outs.transpose(1, 0, 2, 3).reshape(C, NLAT, NLON)
    grad_pre = pres.transpose(1, 0, 2, 3).reshape(C, NLAT, NLON)
    grad_mixing = grad_sum / math.sqrt(NLAT * NLON)
    pre_pad = jnp.pad(grad_pre, ((0, 0), (1, 1), (0, 0)))

    def backward(index):
        start = (index * LAT_DEV).astype(jnp.int32)
        window = lax.dynamic_slice_in_dim(pre_pad, start, LAT_DEV + 2, 1).astype(jnp.float32)
        back = jnp.einsum('okc,olq->kclq', weights, window)
        back = lax.optimization_barrier(back.astype(jnp.bfloat16)).astype(jnp.float32)
        back = wrap_lon(back)
        rows_coef = lax.dynamic_slice_in_dim(coef_pad, start, LAT_DEV + 2, 1)
        acc = jnp.zeros((C, LAT_DEV, NLON), jnp.float32)
        for r in range(3):
            low = 2 - r
            for t in range(taps):
                first = 2 * SMAX - t
                term = rows_coef[:, None, low:low + LAT_DEV, r, t, None] * back[:, :, low:low + LAT_DEV, first:first + NLON]
                acc = acc + lax.optimization_barrier(jnp.sum(term, axis=0))
        cot = lax.dynamic_slice_in_dim(cotangent, start, LAT_DEV, 1).astype(jnp.float32)
        return (cot + acc).astype(jnp.bfloat16)
    grads = lax.map(backward, jnp.arange(blocks, dtype=jnp.int32))
    grad_field = grads.transpose(1, 0, 2, 3).reshape(C, NLAT, NLON)
    return (out_field, grad_field, grad_mixing)
```

```python
import math

import jax
import jax.numpy as jnp
from jax import lax
from jax.sharding import PartitionSpec as P

K = 3
SMAX = 8
TAPS = 2 * SMAX + 1


def swap_edges(first, last, axis, closed):
    count = lax.axis_size(axis)
    odd = lax.axis_index(axis) % 2 == 1
    near = [(j, j ^ 1) for j in range(count)]
    far = []
    for j in range(1, count, 2):
        if closed or j + 1 < count:
            far += [(j, (j + 1) % count), ((j + 1) % count, j)]
    got_near = lax.ppermute(jnp.where(odd, first, last), axis, near)
    got_far = lax.ppermute(jnp.where(odd, last, first), axis, far)
    return jnp.where(odd, got_near, got_far), jnp.where(odd, got_far, got_near)


def gelu_pair(pre):
    root = 0.7978845608028654
    inner = root * (pre + 0.044715 * pre * pre * pre)
    tanh_v = jnp.tanh(inner)
    value = 0.5 * pre * (1.0 + tanh_v)
    slope = 0.5 * (1.0 + tanh_v) + 0.5 * pre * (1.0 - tanh_v * tanh_v) * root * (
        1.0 + 3.0 * 0.044715 * pre * pre
    )
    return (value, slope)


def coef_message(row):
    flat = row.reshape(1, K * 3 * TAPS)
    return jnp.pad(flat, ((0, 15), (0, 256 - K * 3 * TAPS)))


def body(field, cotangent, filters, reach, mixing, bias):
    chans, rows, cols = field.shape
    total_rows = rows * lax.axis_size("lat")
    total_cols = cols * lax.axis_size("lon")
    offsets = jnp.arange(TAPS, dtype=jnp.int32) - SMAX
    inside = (reach[:, 0:1] <= offsets[None, :]) & (offsets[None, :] <= reach[:, 1:2])
    coef = filters * inside[None, :, None, :].astype(jnp.bfloat16)
    field_t = jnp.transpose(field, (1, 2, 0))
    cot_t = jnp.transpose(cotangent, (1, 2, 0))
    two, one = 2 * SMAX, SMAX
    left, right = swap_edges(
        jnp.concatenate([field_t[:, :two], cot_t[:, :one]], axis=1),
        jnp.concatenate([field_t[:, cols - two :], cot_t[:, cols - one :]], axis=1),
        "lon",
        True,
    )
    wide_f = cols + 2 * two
    wide_c = cols + 2 * one
    fx = jnp.concatenate([left[:, :two], field_t, right[:, :two]], axis=1)
    cx = jnp.concatenate([left[:, two:], cot_t, right[:, two:]], axis=1)
    above, below = swap_edges(
        jnp.concatenate(
            [fx[:2].reshape(2 * wide_f, chans), cx[0], coef_message(coef[:, 0])], axis=0
        ),
        jnp.concatenate(
            [
                fx[rows - 2 :].reshape(2 * wide_f, chans),
                cx[rows - 1],
                coef_message(coef[:, rows - 1]),
            ],
            axis=0,
        ),
        "lat",
        False,
    )

    def parts(block):
        f = block[: 2 * wide_f].reshape(2, wide_f, chans)
        c = block[2 * wide_f : 2 * wide_f + wide_c][None]
        k = block[2 * wide_f + wide_c, : K * 3 * TAPS].reshape(K, 1, 3, TAPS)
        return f, c, k

    f_up, c_up, k_up = parts(above)
    f_dn, c_dn, k_dn = parts(below)
    fx = jnp.concatenate([f_up, fx, f_dn], axis=0)
    cx = jnp.concatenate([c_up, cx, c_dn], axis=0)
    coef = jnp.concatenate([k_up, coef, k_dn], axis=1)

    pos_p = jnp.arange(wide_f, dtype=jnp.int32)[None, :, None]
    pos_q = jnp.arange(wide_c, dtype=jnp.int32)[None, None, :]
    pos_b = jnp.arange(cols, dtype=jnp.int32)[None, None, :]
    tap_ids = jnp.arange(TAPS, dtype=jnp.int32)[:, None, None]
    table = (pos_p - pos_q == tap_ids).astype(jnp.bfloat16)
    mirror = (pos_q.reshape(1, wide_c, 1) - pos_b == 2 * SMAX - tap_ids).astype(jnp.bfloat16)
    tall = rows + 2
    band = jnp.einsum("kldt,tpq->ldkpq", coef, table, preferred_element_type=jnp.float32).astype(
        jnp.bfloat16
    )
    acc = 0.0
    for r in range(3):
        acc = acc + jnp.einsum(
            "lpc,lkpq->klqc", fx[r : r + tall], band[:, r], preferred_element_type=jnp.float32
        )
    basis = acc.astype(jnp.bfloat16)
    pre = (
        jnp.einsum("okc,klqc->lqo", mixing, basis, preferred_element_type=jnp.float32)
        + bias[None, None, :]
    )
    value, slope = gelu_pair(pre)
    grad_pre = (cx.astype(jnp.float32) * slope).astype(jnp.bfloat16)
    out_t = (field_t.astype(jnp.float32) + value[1:-1, one : one + cols]).astype(jnp.bfloat16)

    scale = 1.0 / math.sqrt(total_rows * total_cols)
    n_lon, n_lat = lax.axis_size("lon"), lax.axis_size("lat")
    share = chans // n_lon
    term = (
        jnp.einsum(
            "lqo,klqc->okc",
            grad_pre[1:-1, one : one + cols],
            basis[:, 1:-1, one : one + cols],
            preferred_element_type=jnp.float32,
        )
        * scale
    ).astype(jnp.bfloat16)
    got = lax.all_to_all(term.reshape(n_lon, share, K * chans), "lon", 0, 0)
    part = jnp.sum(got.astype(jnp.float32), axis=0).astype(jnp.bfloat16)
    got = lax.all_to_all(jnp.broadcast_to(part[None], (n_lat, share, K * chans)), "lat", 0, 0)
    grad_mixing = jnp.sum(got.astype(jnp.float32), axis=0).reshape(share, K, chans)

    spread = 0.0
    for r in range(3):
        low = 2 - r
        mband = jnp.einsum(
            "klt,tqb->lkqb", coef[:, low : low + rows, r], mirror, preferred_element_type=jnp.float32
        ).astype(jnp.bfloat16)
        spread = spread + jnp.einsum(
            "lqo,lkqb->klbo",
            grad_pre[low : low + rows],
            mband,
            preferred_element_type=jnp.float32,
        )
    inner = jnp.einsum(
        "okc,klbo->lbc", mixing, spread.astype(jnp.bfloat16), preferred_element_type=jnp.float32
    )
    grad_t = (cot_t.astype(jnp.float32) + inner).astype(jnp.bfloat16)
    return (jnp.transpose(out_t, (2, 0, 1)), jnp.transpose(grad_t, (2, 0, 1)), grad_mixing)


def solution(mesh):
    placed = (
        P(None, "lat", "lon"),
        P(None, "lat", "lon"),
        P(None, "lat", None, None),
        P("lat", None),
        P(),
        P(),
    )
    return jax.shard_map(
        body,
        mesh=mesh,
        in_specs=placed,
        out_specs=(P(None, "lat", "lon"), P(None, "lat", "lon"), P("lon", None, None)),
        check_vma=False,
    )
```

```python
import math

import jax
import jax.numpy as jnp
from jax import lax
from jax.experimental import pallas as pl
from jax.experimental.pallas import tpu as pltpu
from jax.sharding import PartitionSpec as P

K = 3
SMAX = 8
TAPS = 2 * SMAX + 1

CELL = 256
ROWS = 16
COLS = 128
TALL = ROWS + 2
WIDE = COLS + 2 * SMAX
LINES = 2 * COLS + 4 * 2 * SMAX + COLS + 2 * SMAX + 16
F32, BF16 = jnp.float32, jnp.bfloat16


def gelu_pair(pre):
    root = 0.7978845608028654
    inner = root * (pre + 0.044715 * pre * pre * pre)
    tanh_v = jnp.tanh(inner)
    value = 0.5 * pre * (1.0 + tanh_v)
    slope = 0.5 * (1.0 + tanh_v) + 0.5 * pre * (1.0 - tanh_v * tanh_v) * root * (
        1.0 + 3.0 * 0.044715 * pre * pre
    )
    return (value, slope)


def toeplitz(line):
    return pltpu.roll(
        jnp.broadcast_to(line, (COLS, COLS)), COLS - SMAX, axis=1, stride=1, stride_axis=0
    )


def halves(cyclic, low):
    first, last = cyclic[:SMAX], cyclic[COLS - SMAX :]
    return (
        jnp.where(low, first, 0.0),
        jnp.where(low, 0.0, first),
        jnp.where(low, last, 0.0),
        jnp.where(low, 0.0, last),
    )


def dot(a, b):
    return jnp.dot(a, b, preferred_element_type=F32)


def rows_of(start, count):
    return pl.ds(pl.multiple_of(start, 16), count)


def forward_kernel(
    odd_ref, near, far, field, field_side, cot, cot_side, taps, mix, bias, scale_ref,
    out, term, grad_main, grad_side, taps_all,
    xm, xs, cm, cs, tap32, band, basis,
):
    def put(block, first_row):
        at = 0
        for ref, size, where in (
            (xm, 2 * COLS, 0 if first_row else TALL * COLS),
            (xs, 4 * 2 * SMAX, 0 if first_row else TALL * 4 * SMAX),
            (cm, COLS, 0 if first_row else (TALL - 1) * COLS),
            (cs, 2 * SMAX, 0 if first_row else (TALL - 1) * 2 * SMAX),
            (taps_all, 16, 0 if first_row else (TALL - 1) * 16),
        ):
            ref[where : where + size, :] = block[at : at + size, :]
            at += size

    @pl.when(odd_ref[0] == 1)
    def _():
        put(near, True)
        put(far, False)

    @pl.when(odd_ref[0] == 0)
    def _():
        put(far, True)
        put(near, False)

    xm[2 * COLS : 2 * COLS + ROWS * COLS, :] = field[...]
    xs[8 * SMAX : 8 * SMAX + ROWS * 4 * SMAX, :] = field_side[...]
    xs[(ROWS + 4) * 4 * SMAX :, :] = jnp.zeros((4 * SMAX, CELL), BF16)
    cm[COLS : COLS + ROWS * COLS, :] = cot[...]
    cs[2 * SMAX : 2 * SMAX + ROWS * 2 * SMAX, :] = cot_side[...]
    taps_all[16 : 16 + ROWS * 16, :] = taps[...]
    tap32[...] = taps_all[:, :COLS].astype(F32)
    grad_side[TALL * 2 * SMAX :, :] = jnp.zeros((5 * 2 * SMAX, CELL), BF16)
    band[...] = jnp.zeros(band.shape, BF16)
    low = lax.broadcasted_iota(jnp.int32, (SMAX, COLS), 1) < COLS // 2
    empty = jnp.zeros((SMAX, COLS), F32)

    def build(row, slot):
        lines = tap32[rows_of(row * 16, 16), :]
        for k in range(K):
            at = k * WIDE
            sides = [empty] * 4
            for r in range(3):
                j = k * 3 + r
                cyclic = toeplitz(lines[j : j + 1, :])
                first_lo, first_hi, last_lo, last_hi = halves(cyclic, low)
                to = slice(r * COLS, (r + 1) * COLS)
                band[slot, at : at + COLS, to] = jnp.concatenate(
                    [first_lo, cyclic[SMAX : COLS - SMAX], last_hi], axis=0
                ).astype(BF16)
                band[slot, at + COLS : at + WIDE, to] = jnp.concatenate(
                    [last_lo, first_hi], axis=0
                ).astype(BF16)
                sides = [
                    have + pltpu.roll(part, 16 + 32 * r, axis=1)
                    for have, part in zip(sides, (first_hi, last_lo, last_hi, first_lo))
                ]
            to = slice(3 * COLS, 4 * COLS)
            band[slot, at : at + 16, to] = jnp.concatenate([sides[0], empty], 0).astype(BF16)
            band[slot, at + COLS - 16 : at + COLS, to] = jnp.concatenate(
                [empty, sides[1]], 0
            ).astype(BF16)
            band[slot, at + COLS : at + WIDE, to] = jnp.concatenate(
                [sides[2], sides[3]], 0
            ).astype(BF16)

    def step(row, carry):
        slot = lax.rem(row, 2)
        build(row, slot)
        cells = jnp.concatenate(
            [xm[rows_of(row * COLS, 3 * COLS), :], xs[rows_of(row * 32, COLS), :]], axis=0
        )
        made = dot(band[slot], cells).astype(BF16)
        wide = jnp.concatenate([made[k * WIDE : (k + 1) * WIDE] for k in range(K)], axis=1)
        pre = dot(wide, mix[...]) + bias[...]
        value, slope = gelu_pair(pre)
        main = rows_of(row * COLS, COLS)
        side = rows_of(row * 16, 16)
        basis[main, :] = wide[:COLS]
        grad_main[main, :] = (cm[main, :].astype(F32) * slope[:COLS]).astype(BF16)
        grad_side[side, :] = (cs[side, :].astype(F32) * slope[COLS:]).astype(BF16)

        @pl.when(jnp.logical_and(row > 0, row < TALL - 1))
        def _():
            out[rows_of((row - 1) * COLS, COLS), :] = (
                xm[rows_of((row + 1) * COLS, COLS), :].astype(F32) + value[:COLS]
            ).astype(BF16)

        return carry

    lax.fori_loop(0, TALL, step, 0)
    total = lax.dot_general(
        grad_main[COLS : COLS + ROWS * COLS, :],
        basis[COLS : COLS + ROWS * COLS, :],
        (((0,), (0,)), ((), ())),
        preferred_element_type=F32,
    )
    term[...] = (total * scale_ref[0]).astype(BF16)


def backward_kernel(grad_main, grad_side, taps_all, mix, cot, out, tap32, band):
    tap32[...] = taps_all[:, COLS:].astype(F32)
    band[...] = jnp.zeros(band.shape, BF16)
    low = lax.broadcasted_iota(jnp.int32, (SMAX, COLS), 1) < COLS // 2
    empty = jnp.zeros((SMAX, COLS), F32)

    def step(row, carry):
        slot = lax.rem(row, 2)
        lines = tap32[rows_of(row * 16, 3 * 16), :]
        for k in range(K):
            at = k * COLS
            sides = [empty] * 2
            for i in range(3):
                j = i * 16 + k * 3 + 2 - i
                cyclic = toeplitz(lines[j : j + 1, :])
                first_lo, first_hi, last_lo, last_hi = halves(cyclic, low)
                band[slot, at : at + COLS, i * COLS : (i + 1) * COLS] = jnp.concatenate(
                    [first_lo, cyclic[SMAX : COLS - SMAX], last_hi], axis=0
                ).astype(BF16)
                sides = [
                    have + pltpu.roll(part, 8 + 16 * i, axis=1)
                    for have, part in zip(sides, (first_hi, last_lo))
                ]
            to = slice(3 * COLS, 4 * COLS)
            band[slot, at : at + 16, to] = jnp.concatenate([sides[0], empty], 0).astype(BF16)
            band[slot, at + COLS - 16 : at + COLS, to] = jnp.concatenate(
                [empty, sides[1]], 0
            ).astype(BF16)
        cells = jnp.concatenate(
            [grad_main[rows_of(row * COLS, 3 * COLS), :], grad_side[rows_of(row * 16, COLS), :]],
            axis=0,
        )
        spread = dot(band[slot], cells).astype(BF16)
        wide = jnp.concatenate([spread[k * COLS : (k + 1) * COLS] for k in range(K)], axis=1)
        main = rows_of(row * COLS, COLS)
        out[main, :] = (cot[main, :].astype(F32) + dot(wide, mix[...])).astype(BF16)
        return carry

    lax.fori_loop(0, ROWS, step, 0)


VMEM = pl.BlockSpec(memory_space=pltpu.VMEM)
SMEM = pl.BlockSpec(memory_space=pltpu.SMEM)


def shape(*sizes):
    return jax.ShapeDtypeStruct(sizes, BF16)


def forward(*operands):
    return pl.pallas_call(
        forward_kernel,
        out_shape=(
            shape(ROWS * COLS, CELL),
            shape(CELL, K * CELL),
            shape(TALL * COLS, CELL),
            shape((TALL + 5) * 16, CELL),
            shape(TALL * 16, CELL),
        ),
        in_specs=[SMEM] + [VMEM] * 9 + [SMEM],
        out_specs=(VMEM,) * 5,
        scratch_shapes=[
            pltpu.VMEM(((ROWS + 4) * COLS, CELL), BF16),
            pltpu.VMEM(((ROWS + 5) * 32, CELL), BF16),
            pltpu.VMEM((TALL * COLS, CELL), BF16),
            pltpu.VMEM((TALL * 16, CELL), BF16),
            pltpu.VMEM((TALL * 16, COLS), F32),
            pltpu.VMEM((2, K * WIDE, 4 * COLS), BF16),
            pltpu.VMEM((TALL * COLS, K * CELL), BF16),
        ],
        compiler_params=pltpu.CompilerParams(vmem_limit_bytes=40 * 2**20),
        cost_estimate=pl.CostEstimate(
            flops=5 * 10**9, bytes_accessed=8 * 10**6, transcendentals=600000
        ),
        name="forward",
    )(*operands)


def backward(*operands):
    return pl.pallas_call(
        backward_kernel,
        out_shape=shape(ROWS * COLS, CELL),
        in_specs=[VMEM] * 5,
        out_specs=VMEM,
        scratch_shapes=[
            pltpu.VMEM((TALL * 16, COLS), F32),
            pltpu.VMEM((2, K * COLS, 4 * COLS), BF16),
        ],
        compiler_params=pltpu.CompilerParams(vmem_limit_bytes=40 * 2**20),
        cost_estimate=pl.CostEstimate(
            flops=3 * 10**9, bytes_accessed=5 * 10**6, transcendentals=0
        ),
        name="backward",
    )(*operands)


def swap_pairs(first, last, axis, closed):
    count = lax.axis_size(axis)
    odd = lax.axis_index(axis) % 2 == 1
    near = [(j, j ^ 1) for j in range(count)]
    far = []
    for j in range(1, count, 2):
        if closed or j + 1 < count:
            far += [(j, (j + 1) % count), ((j + 1) % count, j)]
    got_near = lax.ppermute(jnp.where(odd, first, last), axis, near)
    got_far = lax.ppermute(jnp.where(odd, last, first), axis, far)
    return odd, got_near, got_far


def body(field, cotangent, filters, reach, mixing, bias):
    chans, rows, cols = field.shape
    total_rows = rows * lax.axis_size("lat")
    total_cols = cols * lax.axis_size("lon")
    n_lon, n_lat = lax.axis_size("lon"), lax.axis_size("lat")
    offsets = jnp.arange(TAPS, dtype=jnp.int32) - SMAX
    inside = (reach[:, 0:1] <= offsets[None, :]) & (offsets[None, :] <= reach[:, 1:2])
    coef = filters * inside[None, :, None, :].astype(BF16)
    lines = jnp.transpose(coef, (1, 0, 2, 3)).reshape(rows, K * 3, TAPS)
    lines = jnp.pad(lines, ((0, 0), (0, 16 - K * 3), (0, COLS - TAPS)))
    back = jnp.transpose(coef[..., ::-1], (1, 0, 2, 3)).reshape(rows, K * 3, TAPS)
    back = jnp.pad(back, ((0, 0), (0, 16 - K * 3), (0, COLS - TAPS)))
    taps = jnp.concatenate([lines, back], axis=2)

    field_t = jnp.transpose(field, (1, 2, 0))
    cot_t = jnp.transpose(cotangent, (1, 2, 0))
    two, one = 2 * SMAX, SMAX
    odd, near, far = swap_pairs(
        jnp.concatenate([field_t[:, :two], cot_t[:, :one]], axis=1),
        jnp.concatenate([field_t[:, cols - two :], cot_t[:, cols - one :]], axis=1),
        "lon",
        True,
    )
    left, right = jnp.where(odd, near, far), jnp.where(odd, far, near)
    field_side = jnp.concatenate([left[:, :two], right[:, :two]], axis=1)
    cot_side = jnp.concatenate([left[:, two:], right[:, two:]], axis=1)

    def message(two_rows, row):
        return jnp.concatenate(
            [
                field_t[two_rows].reshape(2 * cols, chans),
                field_side[two_rows].reshape(4 * two, chans),
                cot_t[row],
                cot_side[row],
                taps[row],
            ],
            axis=0,
        )

    odd, near, far = swap_pairs(
        message(slice(0, 2), 0), message(slice(rows - 2, rows), rows - 1), "lat", False
    )
    scale = 1.0 / math.sqrt(total_rows * total_cols)
    cot_lines = cot_t.reshape(rows * cols, chans)
    out_t, term, grad_main, grad_side, taps_all = forward(
        odd.astype(jnp.int32).reshape(1),
        near,
        far,
        field_t.reshape(rows * cols, chans),
        field_side.reshape(rows * 2 * two, chans),
        cot_lines,
        cot_side.reshape(rows * two, chans),
        taps.reshape(rows * 16, chans),
        jnp.transpose(mixing, (1, 2, 0)).reshape(K * chans, chans),
        bias.reshape(1, chans),
        jnp.full((1,), scale, F32),
    )
    share = chans // n_lon
    got = lax.all_to_all(term.reshape(n_lon, share, K * chans), "lon", 0, 0)
    part = jnp.sum(got.astype(F32), axis=0).astype(BF16)
    got = lax.all_to_all(jnp.broadcast_to(part[None], (n_lat, share, K * chans)), "lat", 0, 0)
    grad_mixing = jnp.sum(got.astype(F32), axis=0).reshape(share, K, chans)
    grad_t = backward(
        grad_main,
        grad_side,
        taps_all,
        jnp.transpose(mixing, (1, 0, 2)).reshape(K * chans, chans),
        cot_lines,
    )
    return (
        jnp.transpose(out_t.reshape(rows, cols, chans), (2, 0, 1)),
        jnp.transpose(grad_t.reshape(rows, cols, chans), (2, 0, 1)),
        grad_mixing,
    )


def solution(mesh):
    placed = (
        P(None, "lat", "lon"),
        P(None, "lat", "lon"),
        P(None, "lat", None, None),
        P("lat", None),
        P(),
        P(),
    )
    return jax.shard_map(
        body,
        mesh=mesh,
        in_specs=placed,
        out_specs=(P(None, "lat", "lon"), P(None, "lat", "lon"), P("lon", None, None)),
        check_vma=False,
    )
```

```python
import math

import jax
import jax.numpy as jnp
from jax import lax
from jax.experimental import pallas as pl
from jax.experimental.pallas import tpu as pltpu
from jax.sharding import PartitionSpec as P

K = 3
SMAX = 8
TAPS = 2 * SMAX + 1

CELL = 256
ROWS = 16
COLS = 128
TALL = ROWS + 2
WIDE = COLS + 2 * SMAX
PACK = 6
BACK_PACK = 8
LINES = 2 * COLS + 4 * 2 * SMAX + COLS + 2 * SMAX + 16
F32, BF16 = jnp.float32, jnp.bfloat16


def gelu_pair(pre):
    root = 0.7978845608028654
    inner = root * (pre + 0.044715 * pre * pre * pre)
    tanh_v = jnp.tanh(inner)
    value = 0.5 * pre * (1.0 + tanh_v)
    slope = 0.5 * (1.0 + tanh_v) + 0.5 * pre * (1.0 - tanh_v * tanh_v) * root * (
        1.0 + 3.0 * 0.044715 * pre * pre
    )
    return (value, slope)


def toeplitz(line):
    return pltpu.roll(
        jnp.broadcast_to(line, (COLS, COLS)), COLS - SMAX, axis=1, stride=1, stride_axis=0
    )


def halves(cyclic, low):
    first, last = cyclic[:SMAX], cyclic[COLS - SMAX :]
    return (
        jnp.where(low, first, 0.0),
        jnp.where(low, 0.0, first),
        jnp.where(low, last, 0.0),
        jnp.where(low, 0.0, last),
    )


def dot(a, b):
    return jnp.dot(a, b, preferred_element_type=F32)


def rows_of(start, count):
    return pl.ds(pl.multiple_of(start, 16), count)


def forward_kernel(
    odd_ref, near, far, field, field_side, cot, cot_side, taps, mix_in, bias, scale_ref,
    out_hbm, term_hbm, grad_main_hbm, grad_side_hbm, taps_hbm,
    xm, xs, cm, cs, tap32, band, basis, basis_side, out, term, grad_main, grad_side, taps_all, mix,
    sem_own, sem_near, sem_far, sem_out,
):
    def edges(block, first_row, sems):
        at, copies = 0, []
        for i, (ref, size, where) in enumerate(
            (
                (xm, 2 * COLS, 0 if first_row else TALL * COLS),
                (xs, 4 * 2 * SMAX, 0 if first_row else TALL * 4 * SMAX),
                (cm, COLS, 0 if first_row else (TALL - 1) * COLS),
                (cs, 2 * SMAX, 0 if first_row else (TALL - 1) * 2 * SMAX),
                (taps_all, 16, 0 if first_row else (TALL - 1) * 16),
            )
        ):
            copies.append(
                pltpu.make_async_copy(
                    block.at[pl.ds(at, size)], ref.at[pl.ds(where, size)], sems.at[i]
                )
            )
            at += size
        return copies

    own = [
        pltpu.make_async_copy(src, dst, sem_own.at[i])
        for i, (src, dst) in enumerate(
            (
                (taps, taps_all.at[pl.ds(16, ROWS * 16)]),
                (field, xm.at[pl.ds(2 * COLS, ROWS * COLS)]),
                (field_side, xs.at[pl.ds(8 * SMAX, ROWS * 4 * SMAX)]),
                (cot, cm.at[pl.ds(COLS, ROWS * COLS)]),
                (cot_side, cs.at[pl.ds(2 * SMAX, ROWS * 2 * SMAX)]),
                (mix_in, mix),
            )
        )
    ]
    odd = odd_ref[0] == 1
    even = odd_ref[0] == 0

    @pl.when(odd)
    def _():
        for copy in edges(near, True, sem_near) + edges(far, False, sem_far):
            copy.start()

    @pl.when(even)
    def _():
        for copy in edges(far, True, sem_far) + edges(near, False, sem_near):
            copy.start()

    for copy in own:
        copy.start()
    band[...] = jnp.zeros(band.shape, BF16)
    xs[(ROWS + 4) * 4 * SMAX :, :] = jnp.zeros((4 * SMAX, CELL), BF16)

    @pl.when(odd)
    def _():
        for copy in edges(near, True, sem_near) + edges(far, False, sem_far):
            copy.wait()

    @pl.when(even)
    def _():
        for copy in edges(far, True, sem_far) + edges(near, False, sem_near):
            copy.wait()

    for copy in own:
        copy.wait()
    tap32[...] = taps_all[:, :COLS].astype(F32)
    grad_side[TALL * 2 * SMAX :, :] = jnp.zeros((7 * 2 * SMAX, CELL), BF16)
    low = lax.broadcasted_iota(jnp.int32, (SMAX, COLS), 1) < COLS // 2
    empty = jnp.zeros((SMAX, COLS), F32)

    def build(row, slot):
        lines = tap32[rows_of(row * 16, 16), :]
        for k in range(K):
            at = k * WIDE
            sides = [empty] * 4
            for r in range(3):
                j = k * 3 + r
                cyclic = toeplitz(lines[j : j + 1, :])
                first_lo, first_hi, last_lo, last_hi = halves(cyclic, low)
                to = slice(r * COLS, (r + 1) * COLS)
                band[slot, at : at + COLS, to] = jnp.concatenate(
                    [first_lo, cyclic[SMAX : COLS - SMAX], last_hi], axis=0
                ).astype(BF16)
                band[slot, at + COLS : at + WIDE, to] = jnp.concatenate(
                    [last_lo, first_hi], axis=0
                ).astype(BF16)
                sides = [
                    have + pltpu.roll(part, 16 + 32 * r, axis=1)
                    for have, part in zip(sides, (first_hi, last_lo, last_hi, first_lo))
                ]
            to = slice(3 * COLS, 4 * COLS)
            band[slot, at : at + 16, to] = jnp.concatenate([sides[0], empty], 0).astype(BF16)
            band[slot, at + COLS - 16 : at + COLS, to] = jnp.concatenate(
                [empty, sides[1]], 0
            ).astype(BF16)
            band[slot, at + COLS : at + WIDE, to] = jnp.concatenate(
                [sides[2], sides[3]], 0
            ).astype(BF16)

    def step(group, carry):
        first = group * PACK
        for i in range(PACK):
            row = first + i
            build(row, i)
            cells = jnp.concatenate(
                [xm[rows_of(row * COLS, 3 * COLS), :], xs[rows_of(row * 32, COLS), :]], axis=0
            )
            made = dot(band[i], cells).astype(BF16)
            for k in range(K):
                to = slice(k * CELL, (k + 1) * CELL)
                basis[rows_of(row * COLS, COLS), to] = made[k * WIDE : k * WIDE + COLS]
                basis_side[i * 16 : (i + 1) * 16, to] = made[k * WIDE + COLS : (k + 1) * WIDE]
        main = rows_of(first * COLS, PACK * COLS)
        side = rows_of(first * 16, PACK * 16)
        value, slope = gelu_pair(dot(basis[main, :], mix[...]) + bias[...])
        grad_main[main, :] = (cm[main, :].astype(F32) * slope).astype(BF16)
        here = xm[rows_of((first + 1) * COLS, PACK * COLS), :].astype(F32)
        out[main, :] = (here + value).astype(BF16)
        slope = gelu_pair(dot(basis_side[...], mix[...]) + bias[...])[1]
        grad_side[side, :] = (cs[side, :].astype(F32) * slope).astype(BF16)
        return carry

    lax.fori_loop(0, TALL // PACK, step, 0)
    results = [
        pltpu.make_async_copy(src, dst, sem_out.at[i])
        for i, (src, dst) in enumerate(
            (
                (out.at[pl.ds(COLS, ROWS * COLS)], out_hbm),
                (grad_main, grad_main_hbm),
                (grad_side, grad_side_hbm),
                (taps_all, taps_hbm),
                (term, term_hbm),
            )
        )
    ]
    for copy in results[:4]:
        copy.start()
    total = lax.dot_general(
        grad_main[COLS : COLS + ROWS * COLS, :],
        basis[COLS : COLS + ROWS * COLS, :],
        (((0,), (0,)), ((), ())),
        preferred_element_type=F32,
    )
    term[...] = (total * scale_ref[0]).astype(BF16)
    results[4].start()
    for copy in results:
        copy.wait()


def backward_kernel(
    grad_main_hbm, grad_side_hbm, taps_hbm, mix_hbm, cot_hbm, out_hbm,
    tap32, band, spread, grad_main, grad_side, taps_all, mix, cot, out, sem,
):
    loads = [
        pltpu.make_async_copy(src, dst, sem.at[i])
        for i, (src, dst) in enumerate(
            (
                (taps_hbm, taps_all),
                (grad_main_hbm, grad_main),
                (grad_side_hbm, grad_side),
                (mix_hbm, mix),
                (cot_hbm, cot),
            )
        )
    ]
    for copy in loads:
        copy.start()
    band[...] = jnp.zeros(band.shape, BF16)
    for copy in loads:
        copy.wait()
    tap32[...] = taps_all[:, COLS:].astype(F32)
    low = lax.broadcasted_iota(jnp.int32, (SMAX, COLS), 1) < COLS // 2
    empty = jnp.zeros((SMAX, COLS), F32)

    def build(row, slot):
        lines = tap32[rows_of(row * 16, 3 * 16), :]
        for k in range(K):
            at = k * COLS
            sides = [empty] * 2
            for i in range(3):
                j = i * 16 + k * 3 + 2 - i
                cyclic = toeplitz(lines[j : j + 1, :])
                first_lo, first_hi, last_lo, last_hi = halves(cyclic, low)
                band[slot, at : at + COLS, i * COLS : (i + 1) * COLS] = jnp.concatenate(
                    [first_lo, cyclic[SMAX : COLS - SMAX], last_hi], axis=0
                ).astype(BF16)
                sides = [
                    have + pltpu.roll(part, 8 + 16 * i, axis=1)
                    for have, part in zip(sides, (first_hi, last_lo))
                ]
            to = slice(3 * COLS, 4 * COLS)
            band[slot, at : at + 16, to] = jnp.concatenate([sides[0], empty], 0).astype(BF16)
            band[slot, at + COLS - 16 : at + COLS, to] = jnp.concatenate(
                [empty, sides[1]], 0
            ).astype(BF16)

    def step(group, carry):
        first = group * BACK_PACK
        for i in range(BACK_PACK):
            row = first + i
            build(row, i)
            cells = jnp.concatenate(
                [
                    grad_main[rows_of(row * COLS, 3 * COLS), :],
                    grad_side[rows_of(row * 16, COLS), :],
                ],
                axis=0,
            )
            made = dot(band[i], cells).astype(BF16)
            for k in range(K):
                spread[i * COLS : (i + 1) * COLS, k * CELL : (k + 1) * CELL] = made[
                    k * COLS : (k + 1) * COLS
                ]
        main = rows_of(first * COLS, BACK_PACK * COLS)
        out[main, :] = (cot[main, :].astype(F32) + dot(spread[...], mix[...])).astype(BF16)
        return carry

    lax.fori_loop(0, ROWS // BACK_PACK, step, 0)
    copy = pltpu.make_async_copy(out, out_hbm, sem.at[5])
    copy.start()
    copy.wait()


VMEM = pl.BlockSpec(memory_space=pltpu.VMEM)
HBM = pl.BlockSpec(memory_space=pl.ANY)
SMEM = pl.BlockSpec(memory_space=pltpu.SMEM)


def shape(*sizes):
    return jax.ShapeDtypeStruct(sizes, BF16)


def forward(*operands):
    return pl.pallas_call(
        forward_kernel,
        out_shape=(
            shape(ROWS * COLS, CELL),
            shape(CELL, K * CELL),
            shape(TALL * COLS, CELL),
            shape((TALL + 7) * 16, CELL),
            shape(TALL * 16, CELL),
        ),
        in_specs=[SMEM] + [HBM] * 8 + [VMEM, SMEM],
        out_specs=(HBM,) * 5,
        scratch_shapes=[
            pltpu.VMEM(((ROWS + 4) * COLS, CELL), BF16),
            pltpu.VMEM(((ROWS + 5) * 32, CELL), BF16),
            pltpu.VMEM((TALL * COLS, CELL), BF16),
            pltpu.VMEM((TALL * 16, CELL), BF16),
            pltpu.VMEM((TALL * 16, COLS), F32),
            pltpu.VMEM((PACK, K * WIDE, 4 * COLS), BF16),
            pltpu.VMEM((TALL * COLS, K * CELL), BF16),
            pltpu.VMEM((PACK * 16, K * CELL), BF16),
            pltpu.VMEM((TALL * COLS, CELL), BF16),
            pltpu.VMEM((CELL, K * CELL), BF16),
            pltpu.VMEM((TALL * COLS, CELL), BF16),
            pltpu.VMEM(((TALL + 7) * 16, CELL), BF16),
            pltpu.VMEM((TALL * 16, CELL), BF16),
            pltpu.VMEM((K * CELL, CELL), BF16),
            pltpu.SemaphoreType.DMA((6,)),
            pltpu.SemaphoreType.DMA((5,)),
            pltpu.SemaphoreType.DMA((5,)),
            pltpu.SemaphoreType.DMA((5,)),
        ],
        compiler_params=pltpu.CompilerParams(vmem_limit_bytes=60 * 2**20),
        cost_estimate=pl.CostEstimate(
            flops=5 * 10**9, bytes_accessed=8 * 10**6, transcendentals=600000
        ),
        name="forward",
    )(*operands)


def backward(*operands):
    return pl.pallas_call(
        backward_kernel,
        out_shape=shape(ROWS * COLS, CELL),
        in_specs=[HBM] * 5,
        out_specs=HBM,
        scratch_shapes=[
            pltpu.VMEM((TALL * 16, COLS), F32),
            pltpu.VMEM((BACK_PACK, K * COLS, 4 * COLS), BF16),
            pltpu.VMEM((BACK_PACK * COLS, K * CELL), BF16),
            pltpu.VMEM((TALL * COLS, CELL), BF16),
            pltpu.VMEM(((TALL + 7) * 16, CELL), BF16),
            pltpu.VMEM((TALL * 16, CELL), BF16),
            pltpu.VMEM((K * CELL, CELL), BF16),
            pltpu.VMEM((ROWS * COLS, CELL), BF16),
            pltpu.VMEM((ROWS * COLS, CELL), BF16),
            pltpu.SemaphoreType.DMA((6,)),
        ],
        compiler_params=pltpu.CompilerParams(vmem_limit_bytes=60 * 2**20),
        cost_estimate=pl.CostEstimate(
            flops=3 * 10**9, bytes_accessed=5 * 10**6, transcendentals=0
        ),
        name="backward",
    )(*operands)


def swap_pairs(first, last, axis, closed):
    count = lax.axis_size(axis)
    odd = lax.axis_index(axis) % 2 == 1
    near = [(j, j ^ 1) for j in range(count)]
    far = []
    for j in range(1, count, 2):
        if closed or j + 1 < count:
            far += [(j, (j + 1) % count), ((j + 1) % count, j)]
    got_near = lax.ppermute(jnp.where(odd, first, last), axis, near)
    got_far = lax.ppermute(jnp.where(odd, last, first), axis, far)
    return odd, got_near, got_far


def body(field, cotangent, filters, reach, mixing, bias):
    chans, rows, cols = field.shape
    total_rows = rows * lax.axis_size("lat")
    total_cols = cols * lax.axis_size("lon")
    n_lon, n_lat = lax.axis_size("lon"), lax.axis_size("lat")
    offsets = jnp.arange(TAPS, dtype=jnp.int32) - SMAX
    inside = (reach[:, 0:1] <= offsets[None, :]) & (offsets[None, :] <= reach[:, 1:2])
    coef = filters * inside[None, :, None, :].astype(BF16)
    lines = jnp.transpose(coef, (1, 0, 2, 3)).reshape(rows, K * 3, TAPS)
    lines = jnp.pad(lines, ((0, 0), (0, 16 - K * 3), (0, COLS - TAPS)))
    back = jnp.transpose(coef[..., ::-1], (1, 0, 2, 3)).reshape(rows, K * 3, TAPS)
    back = jnp.pad(back, ((0, 0), (0, 16 - K * 3), (0, COLS - TAPS)))
    taps = jnp.concatenate([lines, back], axis=2)

    field_t = jnp.transpose(field, (1, 2, 0))
    cot_t = jnp.transpose(cotangent, (1, 2, 0))
    two, one = 2 * SMAX, SMAX
    odd, near, far = swap_pairs(
        jnp.concatenate([field_t[:, :two], cot_t[:, :one]], axis=1),
        jnp.concatenate([field_t[:, cols - two :], cot_t[:, cols - one :]], axis=1),
        "lon",
        True,
    )
    left, right = jnp.where(odd, near, far), jnp.where(odd, far, near)
    field_side = jnp.concatenate([left[:, :two], right[:, :two]], axis=1)
    cot_side = jnp.concatenate([left[:, two:], right[:, two:]], axis=1)

    def message(two_rows, row):
        return jnp.concatenate(
            [
                field_t[two_rows].reshape(2 * cols, chans),
                field_side[two_rows].reshape(4 * two, chans),
                cot_t[row],
                cot_side[row],
                taps[row],
            ],
            axis=0,
        )

    odd, near, far = swap_pairs(
        message(slice(0, 2), 0), message(slice(rows - 2, rows), rows - 1), "lat", False
    )
    scale = 1.0 / math.sqrt(total_rows * total_cols)
    cot_lines = cot_t.reshape(rows * cols, chans)
    out_t, term, grad_main, grad_side, taps_all = forward(
        odd.astype(jnp.int32).reshape(1),
        near,
        far,
        field_t.reshape(rows * cols, chans),
        field_side.reshape(rows * 2 * two, chans),
        cot_lines,
        cot_side.reshape(rows * two, chans),
        taps.reshape(rows * 16, chans),
        jnp.transpose(mixing, (1, 2, 0)).reshape(K * chans, chans),
        bias.reshape(1, chans),
        jnp.full((1,), scale, F32),
    )
    share = chans // n_lon
    got = lax.all_to_all(term.reshape(n_lon, share, K * chans), "lon", 0, 0)
    grad_t = backward(
        grad_main,
        grad_side,
        taps_all,
        jnp.transpose(mixing, (1, 0, 2)).reshape(K * chans, chans),
        cot_lines,
    )
    part = jnp.sum(got.astype(F32), axis=0).astype(BF16)
    part, grad_t = lax.optimization_barrier((part, grad_t))
    got = lax.all_to_all(jnp.broadcast_to(part[None], (n_lat, share, K * chans)), "lat", 0, 0)
    grad_mixing = jnp.sum(got.astype(F32), axis=0).reshape(share, K, chans)
    return (
        jnp.transpose(out_t.reshape(rows, cols, chans), (2, 0, 1)),
        jnp.transpose(grad_t.reshape(rows, cols, chans), (2, 0, 1)),
        grad_mixing,
    )


def solution(mesh):
    placed = (
        P(None, "lat", "lon"),
        P(None, "lat", "lon"),
        P(None, "lat", None, None),
        P("lat", None),
        P(),
        P(),
    )
    return jax.shard_map(
        body,
        mesh=mesh,
        in_specs=placed,
        out_specs=(P(None, "lat", "lon"), P(None, "lat", "lon"), P("lon", None, None)),
        check_vma=False,
    )
```

```python
import math

import jax
import jax.numpy as jnp
from jax import lax
from jax.experimental import pallas as pl
from jax.experimental.pallas import tpu as pltpu
from jax.sharding import PartitionSpec as P

K = 3
SMAX = 8
TAPS = 2 * SMAX + 1

CELL = 256
ROWS = 16
COLS = 128
TALL = ROWS + 2
WIDE = COLS + 2 * SMAX
PACK = 6
BACK_PACK = 8
LINES = 2 * COLS + 4 * 2 * SMAX + COLS + 2 * SMAX + 16
F32, BF16 = jnp.float32, jnp.bfloat16


def gelu_pair(pre):
    root = 0.7978845608028654
    inner = root * (pre + 0.044715 * pre * pre * pre)
    tanh_v = jnp.tanh(inner)
    value = 0.5 * pre * (1.0 + tanh_v)
    slope = 0.5 * (1.0 + tanh_v) + 0.5 * pre * (1.0 - tanh_v * tanh_v) * root * (
        1.0 + 3.0 * 0.044715 * pre * pre
    )
    return (value, slope)


def toeplitz(line):
    return pltpu.roll(
        jnp.broadcast_to(line, (COLS, COLS)), COLS - SMAX, axis=1, stride=1, stride_axis=0
    )


def halves(cyclic, low):
    first, last = cyclic[:SMAX], cyclic[COLS - SMAX :]
    return (
        jnp.where(low, first, 0.0),
        jnp.where(low, 0.0, first),
        jnp.where(low, last, 0.0),
        jnp.where(low, 0.0, last),
    )


def dot(a, b):
    return jnp.dot(a, b, preferred_element_type=F32)


def rows_of(start, count):
    return pl.ds(pl.multiple_of(start, 16), count)


def forward_kernel(
    odd_ref, near, far, field, field_side, cot, cot_side, taps, mix_in, bias, scale_ref,
    out_hbm, term_hbm, grad_main_hbm, grad_side_hbm, taps_hbm,
    xm, xs, cm, cs, tap32, band, basis, basis_side, out, term, grad_main, grad_side, taps_all, mix,
    sem_own, sem_near, sem_far, sem_out,
):
    def edges(block, first_row, sems):
        at, copies = 0, []
        for i, (ref, size, where) in enumerate(
            (
                (xm, 2 * COLS, 0 if first_row else TALL * COLS),
                (xs, 4 * 2 * SMAX, 0 if first_row else TALL * 4 * SMAX),
                (cm, COLS, 0 if first_row else (TALL - 1) * COLS),
                (cs, 2 * SMAX, 0 if first_row else (TALL - 1) * 2 * SMAX),
                (taps_all, 16, 0 if first_row else (TALL - 1) * 16),
            )
        ):
            copies.append(
                pltpu.make_async_copy(
                    block.at[pl.ds(at, size)], ref.at[pl.ds(where, size)], sems.at[i]
                )
            )
            at += size
        return copies

    own = [
        pltpu.make_async_copy(src, dst, sem_own.at[i])
        for i, (src, dst) in enumerate(
            (
                (taps, taps_all.at[pl.ds(16, ROWS * 16)]),
                (field, xm.at[pl.ds(2 * COLS, ROWS * COLS)]),
                (field_side, xs.at[pl.ds(8 * SMAX, ROWS * 4 * SMAX)]),
                (cot, cm.at[pl.ds(COLS, ROWS * COLS)]),
                (cot_side, cs.at[pl.ds(2 * SMAX, ROWS * 2 * SMAX)]),
                (mix_in, mix),
            )
        )
    ]
    odd = odd_ref[0] == 1
    even = odd_ref[0] == 0

    @pl.when(odd)
    def _():
        for copy in edges(near, True, sem_near) + edges(far, False, sem_far):
            copy.start()

    @pl.when(even)
    def _():
        for copy in edges(far, True, sem_far) + edges(near, False, sem_near):
            copy.start()

    for copy in own:
        copy.start()
    band[...] = jnp.zeros(band.shape, BF16)
    xs[(ROWS + 4) * 4 * SMAX :, :] = jnp.zeros((4 * SMAX, CELL), BF16)

    @pl.when(odd)
    def _():
        for copy in edges(near, True, sem_near) + edges(far, False, sem_far):
            copy.wait()

    @pl.when(even)
    def _():
        for copy in edges(far, True, sem_far) + edges(near, False, sem_near):
            copy.wait()

    for copy in own:
        copy.wait()
    tap32[...] = taps_all[:, :COLS].astype(F32)
    grad_side[TALL * 2 * SMAX :, :] = jnp.zeros((7 * 2 * SMAX, CELL), BF16)
    low = lax.broadcasted_iota(jnp.int32, (SMAX, COLS), 1) < COLS // 2
    empty = jnp.zeros((SMAX, COLS), F32)

    def build(row, slot):
        lines = tap32[rows_of(row * 16, 16), :]
        for k in range(K):
            at = k * WIDE
            sides = [empty] * 4
            for r in range(3):
                j = k * 3 + r
                cyclic = toeplitz(lines[j : j + 1, :])
                first_lo, first_hi, last_lo, last_hi = halves(cyclic, low)
                to = slice(r * COLS, (r + 1) * COLS)
                band[slot, at : at + COLS, to] = jnp.concatenate(
                    [first_lo, cyclic[SMAX : COLS - SMAX], last_hi], axis=0
                ).astype(BF16)
                band[slot, at + COLS : at + WIDE, to] = jnp.concatenate(
                    [last_lo, first_hi], axis=0
                ).astype(BF16)
                sides = [
                    have + pltpu.roll(part, 16 + 32 * r, axis=1)
                    for have, part in zip(sides, (first_hi, last_lo, last_hi, first_lo))
                ]
            to = slice(3 * COLS, 4 * COLS)
            band[slot, at : at + 16, to] = jnp.concatenate([sides[0], empty], 0).astype(BF16)
            band[slot, at + COLS - 16 : at + COLS, to] = jnp.concatenate(
                [empty, sides[1]], 0
            ).astype(BF16)
            band[slot, at + COLS : at + WIDE, to] = jnp.concatenate(
                [sides[2], sides[3]], 0
            ).astype(BF16)

    def step(group, carry):
        first = group * PACK
        for i in range(PACK):
            row = first + i
            build(row, i)
            cells = jnp.concatenate(
                [xm[rows_of(row * COLS, 3 * COLS), :], xs[rows_of(row * 32, COLS), :]], axis=0
            )
            made = dot(band[i], cells).astype(BF16)
            for k in range(K):
                to = slice(k * CELL, (k + 1) * CELL)
                basis[rows_of(row * COLS, COLS), to] = made[k * WIDE : k * WIDE + COLS]
                basis_side[i * 16 : (i + 1) * 16, to] = made[k * WIDE + COLS : (k + 1) * WIDE]
        main = rows_of(first * COLS, PACK * COLS)
        side = rows_of(first * 16, PACK * 16)
        value, slope = gelu_pair(dot(basis[main, :], mix[...]) + bias[...])
        grad_main[main, :] = (cm[main, :].astype(F32) * slope).astype(BF16)
        here = xm[rows_of((first + 1) * COLS, PACK * COLS), :].astype(F32)
        out[main, :] = (here + value).astype(BF16)
        slope = gelu_pair(dot(basis_side[...], mix[...]) + bias[...])[1]
        grad_side[side, :] = (cs[side, :].astype(F32) * slope).astype(BF16)
        return carry

    lax.fori_loop(0, TALL // PACK, step, 0, unroll=True)
    results = [
        pltpu.make_async_copy(src, dst, sem_out.at[i])
        for i, (src, dst) in enumerate(
            (
                (out.at[pl.ds(COLS, ROWS * COLS)], out_hbm),
                (grad_main, grad_main_hbm),
                (grad_side, grad_side_hbm),
                (taps_all, taps_hbm),
                (term, term_hbm),
            )
        )
    ]
    for copy in results[:4]:
        copy.start()
    total = lax.dot_general(
        grad_main[COLS : COLS + ROWS * COLS, :],
        basis[COLS : COLS + ROWS * COLS, :],
        (((0,), (0,)), ((), ())),
        preferred_element_type=F32,
    )
    term[...] = (total * scale_ref[0]).astype(BF16)
    results[4].start()
    for copy in results:
        copy.wait()


def backward_kernel(
    grad_main_hbm, grad_side_hbm, taps_hbm, mix_hbm, cot_hbm, out_hbm,
    tap32, band, spread, grad_main, grad_side, taps_all, mix, cot, out, sem,
):
    loads = [
        pltpu.make_async_copy(src, dst, sem.at[i])
        for i, (src, dst) in enumerate(
            (
                (taps_hbm, taps_all),
                (grad_main_hbm, grad_main),
                (grad_side_hbm, grad_side),
                (mix_hbm, mix),
                (cot_hbm, cot),
            )
        )
    ]
    for copy in loads:
        copy.start()
    band[...] = jnp.zeros(band.shape, BF16)
    for copy in loads:
        copy.wait()
    tap32[...] = taps_all[:, COLS:].astype(F32)
    low = lax.broadcasted_iota(jnp.int32, (SMAX, COLS), 1) < COLS // 2
    empty = jnp.zeros((SMAX, COLS), F32)

    def build(row, slot):
        lines = tap32[rows_of(row * 16, 3 * 16), :]
        for k in range(K):
            at = k * COLS
            sides = [empty] * 2
            for i in range(3):
                j = i * 16 + k * 3 + 2 - i
                cyclic = toeplitz(lines[j : j + 1, :])
                first_lo, first_hi, last_lo, last_hi = halves(cyclic, low)
                band[slot, at : at + COLS, i * COLS : (i + 1) * COLS] = jnp.concatenate(
                    [first_lo, cyclic[SMAX : COLS - SMAX], last_hi], axis=0
                ).astype(BF16)
                sides = [
                    have + pltpu.roll(part, 8 + 16 * i, axis=1)
                    for have, part in zip(sides, (first_hi, last_lo))
                ]
            to = slice(3 * COLS, 4 * COLS)
            band[slot, at : at + 16, to] = jnp.concatenate([sides[0], empty], 0).astype(BF16)
            band[slot, at + COLS - 16 : at + COLS, to] = jnp.concatenate(
                [empty, sides[1]], 0
            ).astype(BF16)

    def step(group, carry):
        first = group * BACK_PACK
        for i in range(BACK_PACK):
            row = first + i
            build(row, i)
            cells = jnp.concatenate(
                [
                    grad_main[rows_of(row * COLS, 3 * COLS), :],
                    grad_side[rows_of(row * 16, COLS), :],
                ],
                axis=0,
            )
            made = dot(band[i], cells).astype(BF16)
            for k in range(K):
                spread[i * COLS : (i + 1) * COLS, k * CELL : (k + 1) * CELL] = made[
                    k * COLS : (k + 1) * COLS
                ]
        main = rows_of(first * COLS, BACK_PACK * COLS)
        out[main, :] = (cot[main, :].astype(F32) + dot(spread[...], mix[...])).astype(BF16)
        return carry

    lax.fori_loop(0, ROWS // BACK_PACK, step, 0)
    copy = pltpu.make_async_copy(out, out_hbm, sem.at[5])
    copy.start()
    copy.wait()


VMEM = pl.BlockSpec(memory_space=pltpu.VMEM)
HBM = pl.BlockSpec(memory_space=pl.ANY)
SMEM = pl.BlockSpec(memory_space=pltpu.SMEM)


def shape(*sizes):
    return jax.ShapeDtypeStruct(sizes, BF16)


def forward(*operands):
    return pl.pallas_call(
        forward_kernel,
        out_shape=(
            shape(ROWS * COLS, CELL),
            shape(CELL, K * CELL),
            shape(TALL * COLS, CELL),
            shape((TALL + 7) * 16, CELL),
            shape(TALL * 16, CELL),
        ),
        in_specs=[SMEM] + [HBM] * 8 + [VMEM, SMEM],
        out_specs=(HBM,) * 5,
        scratch_shapes=[
            pltpu.VMEM(((ROWS + 4) * COLS, CELL), BF16),
            pltpu.VMEM(((ROWS + 5) * 32, CELL), BF16),
            pltpu.VMEM((TALL * COLS, CELL), BF16),
            pltpu.VMEM((TALL * 16, CELL), BF16),
            pltpu.VMEM((TALL * 16, COLS), F32),
            pltpu.VMEM((PACK, K * WIDE, 4 * COLS), BF16),
            pltpu.VMEM((TALL * COLS, K * CELL), BF16),
            pltpu.VMEM((PACK * 16, K * CELL), BF16),
            pltpu.VMEM((TALL * COLS, CELL), BF16),
            pltpu.VMEM((CELL, K * CELL), BF16),
            pltpu.VMEM((TALL * COLS, CELL), BF16),
            pltpu.VMEM(((TALL + 7) * 16, CELL), BF16),
            pltpu.VMEM((TALL * 16, CELL), BF16),
            pltpu.VMEM((K * CELL, CELL), BF16),
            pltpu.SemaphoreType.DMA((6,)),
            pltpu.SemaphoreType.DMA((5,)),
            pltpu.SemaphoreType.DMA((5,)),
            pltpu.SemaphoreType.DMA((5,)),
        ],
        compiler_params=pltpu.CompilerParams(vmem_limit_bytes=60 * 2**20),
        cost_estimate=pl.CostEstimate(
            flops=5 * 10**9, bytes_accessed=8 * 10**6, transcendentals=600000
        ),
        name="forward",
    )(*operands)


def backward(*operands):
    return pl.pallas_call(
        backward_kernel,
        out_shape=shape(ROWS * COLS, CELL),
        in_specs=[HBM] * 5,
        out_specs=HBM,
        scratch_shapes=[
            pltpu.VMEM((TALL * 16, COLS), F32),
            pltpu.VMEM((BACK_PACK, K * COLS, 4 * COLS), BF16),
            pltpu.VMEM((BACK_PACK * COLS, K * CELL), BF16),
            pltpu.VMEM((TALL * COLS, CELL), BF16),
            pltpu.VMEM(((TALL + 7) * 16, CELL), BF16),
            pltpu.VMEM((TALL * 16, CELL), BF16),
            pltpu.VMEM((K * CELL, CELL), BF16),
            pltpu.VMEM((ROWS * COLS, CELL), BF16),
            pltpu.VMEM((ROWS * COLS, CELL), BF16),
            pltpu.SemaphoreType.DMA((6,)),
        ],
        compiler_params=pltpu.CompilerParams(vmem_limit_bytes=60 * 2**20),
        cost_estimate=pl.CostEstimate(
            flops=3 * 10**9, bytes_accessed=5 * 10**6, transcendentals=0
        ),
        name="backward",
    )(*operands)


def swap_pairs(first, last, axis, closed):
    count = lax.axis_size(axis)
    odd = lax.axis_index(axis) % 2 == 1
    near = [(j, j ^ 1) for j in range(count)]
    far = []
    for j in range(1, count, 2):
        if closed or j + 1 < count:
            far += [(j, (j + 1) % count), ((j + 1) % count, j)]
    got_near = lax.ppermute(jnp.where(odd, first, last), axis, near)
    got_far = lax.ppermute(jnp.where(odd, last, first), axis, far)
    return odd, got_near, got_far


def body(field, cotangent, filters, reach, mixing, bias):
    chans, rows, cols = field.shape
    total_rows = rows * lax.axis_size("lat")
    total_cols = cols * lax.axis_size("lon")
    n_lon, n_lat = lax.axis_size("lon"), lax.axis_size("lat")
    offsets = jnp.arange(TAPS, dtype=jnp.int32) - SMAX
    inside = (reach[:, 0:1] <= offsets[None, :]) & (offsets[None, :] <= reach[:, 1:2])
    coef = filters * inside[None, :, None, :].astype(BF16)
    lines = jnp.transpose(coef, (1, 0, 2, 3)).reshape(rows, K * 3, TAPS)
    lines = jnp.pad(lines, ((0, 0), (0, 16 - K * 3), (0, COLS - TAPS)))
    back = jnp.transpose(coef[..., ::-1], (1, 0, 2, 3)).reshape(rows, K * 3, TAPS)
    back = jnp.pad(back, ((0, 0), (0, 16 - K * 3), (0, COLS - TAPS)))
    taps = jnp.concatenate([lines, back], axis=2)

    field_t = jnp.transpose(field, (1, 2, 0))
    cot_t = jnp.transpose(cotangent, (1, 2, 0))
    two, one = 2 * SMAX, SMAX
    odd, near, far = swap_pairs(
        jnp.concatenate([field_t[:, :two], cot_t[:, :one]], axis=1),
        jnp.concatenate([field_t[:, cols - two :], cot_t[:, cols - one :]], axis=1),
        "lon",
        True,
    )
    left, right = jnp.where(odd, near, far), jnp.where(odd, far, near)
    field_side = jnp.concatenate([left[:, :two], right[:, :two]], axis=1)
    cot_side = jnp.concatenate([left[:, two:], right[:, two:]], axis=1)

    def message(two_rows, row):
        return jnp.concatenate(
            [
                field_t[two_rows].reshape(2 * cols, chans),
                field_side[two_rows].reshape(4 * two, chans),
                cot_t[row],
                cot_side[row],
                taps[row],
            ],
            axis=0,
        )

    odd, near, far = swap_pairs(
        message(slice(0, 2), 0), message(slice(rows - 2, rows), rows - 1), "lat", False
    )
    scale = 1.0 / math.sqrt(total_rows * total_cols)
    cot_lines = cot_t.reshape(rows * cols, chans)
    out_t, term, grad_main, grad_side, taps_all = forward(
        odd.astype(jnp.int32).reshape(1),
        near,
        far,
        field_t.reshape(rows * cols, chans),
        field_side.reshape(rows * 2 * two, chans),
        cot_lines,
        cot_side.reshape(rows * two, chans),
        taps.reshape(rows * 16, chans),
        jnp.transpose(mixing, (1, 2, 0)).reshape(K * chans, chans),
        bias.reshape(1, chans),
        jnp.full((1,), scale, F32),
    )
    share = chans // n_lon
    got = lax.all_to_all(term.reshape(n_lon, share, K * chans), "lon", 0, 0)
    grad_t = backward(
        grad_main,
        grad_side,
        taps_all,
        jnp.transpose(mixing, (1, 0, 2)).reshape(K * chans, chans),
        cot_lines,
    )
    part = jnp.sum(got.astype(F32), axis=0).astype(BF16)
    part, grad_t = lax.optimization_barrier((part, grad_t))
    got = lax.all_to_all(jnp.broadcast_to(part[None], (n_lat, share, K * chans)), "lat", 0, 0)
    grad_mixing = jnp.sum(got.astype(F32), axis=0).reshape(share, K, chans)
    return (
        jnp.transpose(out_t.reshape(rows, cols, chans), (2, 0, 1)),
        jnp.transpose(grad_t.reshape(rows, cols, chans), (2, 0, 1)),
        grad_mixing,
    )


def solution(mesh):
    placed = (
        P(None, "lat", "lon"),
        P(None, "lat", "lon"),
        P(None, "lat", None, None),
        P("lat", None),
        P(),
        P(),
    )
    return jax.shard_map(
        body,
        mesh=mesh,
        in_specs=placed,
        out_specs=(P(None, "lat", "lon"), P(None, "lat", "lon"), P("lon", None, None)),
        check_vma=False,
    )
```

```python
import math

import jax
import jax.numpy as jnp
from jax import lax
from jax.experimental import pallas as pl
from jax.experimental.pallas import tpu as pltpu
from jax.sharding import PartitionSpec as P

K = 3
SMAX = 8
TAPS = 2 * SMAX + 1

CELL = 256
ROWS = 16
COLS = 128
TALL = ROWS + 2
WIDE = COLS + 2 * SMAX
PACK = 6
BACK_PACK = 8
LINES = 2 * COLS + 4 * 2 * SMAX + COLS + 2 * SMAX + 16
F32, BF16 = jnp.float32, jnp.bfloat16


def gelu_pair(pre):
    root = 0.7978845608028654
    inner = root * (pre + 0.044715 * pre * pre * pre)
    tanh_v = jnp.tanh(inner)
    value = 0.5 * pre * (1.0 + tanh_v)
    slope = 0.5 * (1.0 + tanh_v) + 0.5 * pre * (1.0 - tanh_v * tanh_v) * root * (
        1.0 + 3.0 * 0.044715 * pre * pre
    )
    return (value, slope)


def toeplitz(line):
    return pltpu.roll(
        jnp.broadcast_to(line, (COLS, COLS)), COLS - SMAX, axis=1, stride=1, stride_axis=0
    )


def halves(cyclic, low):
    first, last = cyclic[:SMAX], cyclic[COLS - SMAX :]
    return (
        jnp.where(low, first, 0.0),
        jnp.where(low, 0.0, first),
        jnp.where(low, last, 0.0),
        jnp.where(low, 0.0, last),
    )


def dot(a, b):
    return jnp.dot(a, b, preferred_element_type=F32)


def rows_of(start, count):
    return pl.ds(pl.multiple_of(start, 16), count)


def forward_kernel(
    odd_ref, near, far, field, field_side, cot, cot_side, taps, mix_in, bias, scale_ref,
    out_hbm, term_hbm, grad_main_hbm, grad_side_hbm, taps_hbm,
    xm, xs, cm, cs, tap32, band, basis, basis_side, out, term, grad_main, grad_side, taps_all, mix,
    sem_own, sem_near, sem_far, sem_out,
):
    def edges(block, first_row, sems):
        at, copies = 0, []
        for i, (ref, size, where) in enumerate(
            (
                (xm, 2 * COLS, 0 if first_row else TALL * COLS),
                (xs, 4 * 2 * SMAX, 0 if first_row else TALL * 4 * SMAX),
                (cm, COLS, 0 if first_row else (TALL - 1) * COLS),
                (cs, 2 * SMAX, 0 if first_row else (TALL - 1) * 2 * SMAX),
                (taps_all, 16, 0 if first_row else (TALL - 1) * 16),
            )
        ):
            copies.append(
                pltpu.make_async_copy(
                    block.at[pl.ds(at, size)], ref.at[pl.ds(where, size)], sems.at[i]
                )
            )
            at += size
        return copies

    own = [
        pltpu.make_async_copy(src, dst, sem_own.at[i])
        for i, (src, dst) in enumerate(
            (
                (taps, taps_all.at[pl.ds(16, ROWS * 16)]),
                (field, xm.at[pl.ds(2 * COLS, ROWS * COLS)]),
                (field_side, xs.at[pl.ds(8 * SMAX, ROWS * 4 * SMAX)]),
                (cot, cm.at[pl.ds(COLS, ROWS * COLS)]),
                (cot_side, cs.at[pl.ds(2 * SMAX, ROWS * 2 * SMAX)]),
                (mix_in, mix),
            )
        )
    ]
    odd = odd_ref[0] == 1
    even = odd_ref[0] == 0

    @pl.when(odd)
    def _():
        for copy in edges(near, True, sem_near) + edges(far, False, sem_far):
            copy.start()

    @pl.when(even)
    def _():
        for copy in edges(far, True, sem_far) + edges(near, False, sem_near):
            copy.start()

    for copy in own:
        copy.start()
    band[...] = jnp.zeros(band.shape, BF16)
    xs[(ROWS + 4) * 4 * SMAX :, :] = jnp.zeros((4 * SMAX, CELL), BF16)

    @pl.when(odd)
    def _():
        for copy in edges(near, True, sem_near) + edges(far, False, sem_far):
            copy.wait()

    @pl.when(even)
    def _():
        for copy in edges(far, True, sem_far) + edges(near, False, sem_near):
            copy.wait()

    for copy in own:
        copy.wait()
    tap32[...] = taps_all[:, :COLS].astype(F32)
    grad_side[TALL * 2 * SMAX :, :] = jnp.zeros((7 * 2 * SMAX, CELL), BF16)
    low = lax.broadcasted_iota(jnp.int32, (SMAX, COLS), 1) < COLS // 2
    empty = jnp.zeros((SMAX, COLS), F32)

    def build(row, slot):
        lines = tap32[rows_of(row * 16, 16), :]
        for k in range(K):
            at = k * WIDE
            sides = [empty] * 4
            for r in range(3):
                j = k * 3 + r
                cyclic = toeplitz(lines[j : j + 1, :])
                first_lo, first_hi, last_lo, last_hi = halves(cyclic, low)
                to = slice(r * COLS, (r + 1) * COLS)
                band[slot, at : at + COLS, to] = jnp.concatenate(
                    [first_lo, cyclic[SMAX : COLS - SMAX], last_hi], axis=0
                ).astype(BF16)
                band[slot, at + COLS : at + WIDE, to] = jnp.concatenate(
                    [last_lo, first_hi], axis=0
                ).astype(BF16)
                sides = [
                    have + pltpu.roll(part, 16 + 32 * r, axis=1)
                    for have, part in zip(sides, (first_hi, last_lo, last_hi, first_lo))
                ]
            to = slice(3 * COLS, 4 * COLS)
            band[slot, at : at + 16, to] = jnp.concatenate([sides[0], empty], 0).astype(BF16)
            band[slot, at + COLS - 16 : at + COLS, to] = jnp.concatenate(
                [empty, sides[1]], 0
            ).astype(BF16)
            band[slot, at + COLS : at + WIDE, to] = jnp.concatenate(
                [sides[2], sides[3]], 0
            ).astype(BF16)

    def step(group, carry):
        first = group * PACK
        for i in range(PACK):
            row = first + i
            build(row, i)
            cells = jnp.concatenate(
                [xm[rows_of(row * COLS, 3 * COLS), :], xs[rows_of(row * 32, COLS), :]], axis=0
            )
            made = dot(band[i], cells).astype(BF16)
            for k in range(K):
                to = slice(k * CELL, (k + 1) * CELL)
                basis[rows_of(row * COLS, COLS), to] = made[k * WIDE : k * WIDE + COLS]
                basis_side[i * 16 : (i + 1) * 16, to] = made[k * WIDE + COLS : (k + 1) * WIDE]
        main = rows_of(first * COLS, PACK * COLS)
        side = rows_of(first * 16, PACK * 16)
        value, slope = gelu_pair(dot(basis[main, :], mix[...]) + bias[...])
        grad_main[main, :] = (cm[main, :].astype(F32) * slope).astype(BF16)
        here = xm[rows_of((first + 1) * COLS, PACK * COLS), :].astype(F32)
        out[main, :] = (here + value).astype(BF16)
        slope = gelu_pair(dot(basis_side[...], mix[...]) + bias[...])[1]
        grad_side[side, :] = (cs[side, :].astype(F32) * slope).astype(BF16)
        return carry

    size = PACK * COLS
    pieces = []
    for group in range(TALL // PACK):
        low_line = max(group * size, COLS)
        high_line = min((group + 1) * size, (TALL - 1) * COLS)
        pieces.append(
            (
                out.at[pl.ds(low_line, high_line - low_line)],
                out_hbm.at[pl.ds(low_line - COLS, high_line - low_line)],
            )
        )
        pieces.append(
            (grad_main.at[pl.ds(group * size, size)], grad_main_hbm.at[pl.ds(group * size, size)])
        )
    pieces += [(grad_side, grad_side_hbm), (taps_all, taps_hbm), (term, term_hbm)]
    results = [
        pltpu.make_async_copy(src, dst, sem_out.at[i]) for i, (src, dst) in enumerate(pieces)
    ]
    for group in range(TALL // PACK):
        step(group, 0)
        for copy in results[2 * group : 2 * group + 2]:
            copy.start()
    for copy in results[-3:-1]:
        copy.start()
    total = lax.dot_general(
        grad_main[COLS : COLS + ROWS * COLS, :],
        basis[COLS : COLS + ROWS * COLS, :],
        (((0,), (0,)), ((), ())),
        preferred_element_type=F32,
    )
    term[...] = (total * scale_ref[0]).astype(BF16)
    results[-1].start()
    for copy in results:
        copy.wait()


def backward_kernel(
    grad_main_hbm, grad_side_hbm, taps_hbm, mix_hbm, cot_hbm, out_hbm,
    tap32, band, spread, grad_main, grad_side, taps_all, mix, cot, out, sem,
):
    loads = [
        pltpu.make_async_copy(src, dst, sem.at[i])
        for i, (src, dst) in enumerate(
            (
                (taps_hbm, taps_all),
                (grad_main_hbm, grad_main),
                (grad_side_hbm, grad_side),
                (mix_hbm, mix),
                (cot_hbm, cot),
            )
        )
    ]
    for copy in loads:
        copy.start()
    band[...] = jnp.zeros(band.shape, BF16)
    for copy in loads:
        copy.wait()
    tap32[...] = taps_all[:, COLS:].astype(F32)
    low = lax.broadcasted_iota(jnp.int32, (SMAX, COLS), 1) < COLS // 2
    empty = jnp.zeros((SMAX, COLS), F32)

    def build(row, slot):
        lines = tap32[rows_of(row * 16, 3 * 16), :]
        for k in range(K):
            at = k * COLS
            sides = [empty] * 2
            for i in range(3):
                j = i * 16 + k * 3 + 2 - i
                cyclic = toeplitz(lines[j : j + 1, :])
                first_lo, first_hi, last_lo, last_hi = halves(cyclic, low)
                band[slot, at : at + COLS, i * COLS : (i + 1) * COLS] = jnp.concatenate(
                    [first_lo, cyclic[SMAX : COLS - SMAX], last_hi], axis=0
                ).astype(BF16)
                sides = [
                    have + pltpu.roll(part, 8 + 16 * i, axis=1)
                    for have, part in zip(sides, (first_hi, last_lo))
                ]
            to = slice(3 * COLS, 4 * COLS)
            band[slot, at : at + 16, to] = jnp.concatenate([sides[0], empty], 0).astype(BF16)
            band[slot, at + COLS - 16 : at + COLS, to] = jnp.concatenate(
                [empty, sides[1]], 0
            ).astype(BF16)

    def step(group, carry):
        first = group * BACK_PACK
        for i in range(BACK_PACK):
            row = first + i
            build(row, i)
            cells = jnp.concatenate(
                [
                    grad_main[rows_of(row * COLS, 3 * COLS), :],
                    grad_side[rows_of(row * 16, COLS), :],
                ],
                axis=0,
            )
            made = dot(band[i], cells).astype(BF16)
            for k in range(K):
                spread[i * COLS : (i + 1) * COLS, k * CELL : (k + 1) * CELL] = made[
                    k * COLS : (k + 1) * COLS
                ]
        main = rows_of(first * COLS, BACK_PACK * COLS)
        out[main, :] = (cot[main, :].astype(F32) + dot(spread[...], mix[...])).astype(BF16)
        return carry

    lax.fori_loop(0, ROWS // BACK_PACK, step, 0)
    copy = pltpu.make_async_copy(out, out_hbm, sem.at[5])
    copy.start()
    copy.wait()


VMEM = pl.BlockSpec(memory_space=pltpu.VMEM)
HBM = pl.BlockSpec(memory_space=pl.ANY)
SMEM = pl.BlockSpec(memory_space=pltpu.SMEM)


def shape(*sizes):
    return jax.ShapeDtypeStruct(sizes, BF16)


def forward(*operands):
    return pl.pallas_call(
        forward_kernel,
        out_shape=(
            shape(ROWS * COLS, CELL),
            shape(CELL, K * CELL),
            shape(TALL * COLS, CELL),
            shape((TALL + 7) * 16, CELL),
            shape(TALL * 16, CELL),
        ),
        in_specs=[SMEM] + [HBM] * 8 + [VMEM, SMEM],
        out_specs=(HBM,) * 5,
        scratch_shapes=[
            pltpu.VMEM(((ROWS + 4) * COLS, CELL), BF16),
            pltpu.VMEM(((ROWS + 5) * 32, CELL), BF16),
            pltpu.VMEM((TALL * COLS, CELL), BF16),
            pltpu.VMEM((TALL * 16, CELL), BF16),
            pltpu.VMEM((TALL * 16, COLS), F32),
            pltpu.VMEM((PACK, K * WIDE, 4 * COLS), BF16),
            pltpu.VMEM((TALL * COLS, K * CELL), BF16),
            pltpu.VMEM((PACK * 16, K * CELL), BF16),
            pltpu.VMEM((TALL * COLS, CELL), BF16),
            pltpu.VMEM((CELL, K * CELL), BF16),
            pltpu.VMEM((TALL * COLS, CELL), BF16),
            pltpu.VMEM(((TALL + 7) * 16, CELL), BF16),
            pltpu.VMEM((TALL * 16, CELL), BF16),
            pltpu.VMEM((K * CELL, CELL), BF16),
            pltpu.SemaphoreType.DMA((6,)),
            pltpu.SemaphoreType.DMA((5,)),
            pltpu.SemaphoreType.DMA((5,)),
            pltpu.SemaphoreType.DMA((9,)),
        ],
        compiler_params=pltpu.CompilerParams(vmem_limit_bytes=60 * 2**20),
        cost_estimate=pl.CostEstimate(
            flops=5 * 10**9, bytes_accessed=8 * 10**6, transcendentals=600000
        ),
        name="forward",
    )(*operands)


def backward(*operands):
    return pl.pallas_call(
        backward_kernel,
        out_shape=shape(ROWS * COLS, CELL),
        in_specs=[HBM] * 5,
        out_specs=HBM,
        scratch_shapes=[
            pltpu.VMEM((TALL * 16, COLS), F32),
            pltpu.VMEM((BACK_PACK, K * COLS, 4 * COLS), BF16),
            pltpu.VMEM((BACK_PACK * COLS, K * CELL), BF16),
            pltpu.VMEM((TALL * COLS, CELL), BF16),
            pltpu.VMEM(((TALL + 7) * 16, CELL), BF16),
            pltpu.VMEM((TALL * 16, CELL), BF16),
            pltpu.VMEM((K * CELL, CELL), BF16),
            pltpu.VMEM((ROWS * COLS, CELL), BF16),
            pltpu.VMEM((ROWS * COLS, CELL), BF16),
            pltpu.SemaphoreType.DMA((6,)),
        ],
        compiler_params=pltpu.CompilerParams(vmem_limit_bytes=60 * 2**20),
        cost_estimate=pl.CostEstimate(
            flops=3 * 10**9, bytes_accessed=5 * 10**6, transcendentals=0
        ),
        name="backward",
    )(*operands)


def swap_pairs(first, last, axis, closed):
    count = lax.axis_size(axis)
    odd = lax.axis_index(axis) % 2 == 1
    near = [(j, j ^ 1) for j in range(count)]
    far = []
    for j in range(1, count, 2):
        if closed or j + 1 < count:
            far += [(j, (j + 1) % count), ((j + 1) % count, j)]
    got_near = lax.ppermute(jnp.where(odd, first, last), axis, near)
    got_far = lax.ppermute(jnp.where(odd, last, first), axis, far)
    return odd, got_near, got_far


def body(field, cotangent, filters, reach, mixing, bias):
    chans, rows, cols = field.shape
    total_rows = rows * lax.axis_size("lat")
    total_cols = cols * lax.axis_size("lon")
    n_lon, n_lat = lax.axis_size("lon"), lax.axis_size("lat")
    offsets = jnp.arange(TAPS, dtype=jnp.int32) - SMAX
    inside = (reach[:, 0:1] <= offsets[None, :]) & (offsets[None, :] <= reach[:, 1:2])
    coef = filters * inside[None, :, None, :].astype(BF16)
    lines = jnp.transpose(coef, (1, 0, 2, 3)).reshape(rows, K * 3, TAPS)
    lines = jnp.pad(lines, ((0, 0), (0, 16 - K * 3), (0, COLS - TAPS)))
    back = jnp.transpose(coef[..., ::-1], (1, 0, 2, 3)).reshape(rows, K * 3, TAPS)
    back = jnp.pad(back, ((0, 0), (0, 16 - K * 3), (0, COLS - TAPS)))
    taps = jnp.concatenate([lines, back], axis=2)

    field_t = jnp.transpose(field, (1, 2, 0))
    cot_t = jnp.transpose(cotangent, (1, 2, 0))
    two, one = 2 * SMAX, SMAX
    odd, near, far = swap_pairs(
        jnp.concatenate([field_t[:, :two], cot_t[:, :one]], axis=1),
        jnp.concatenate([field_t[:, cols - two :], cot_t[:, cols - one :]], axis=1),
        "lon",
        True,
    )
    left, right = jnp.where(odd, near, far), jnp.where(odd, far, near)
    field_side = jnp.concatenate([left[:, :two], right[:, :two]], axis=1)
    cot_side = jnp.concatenate([left[:, two:], right[:, two:]], axis=1)

    def message(two_rows, row):
        return jnp.concatenate(
            [
                field_t[two_rows].reshape(2 * cols, chans),
                field_side[two_rows].reshape(4 * two, chans),
                cot_t[row],
                cot_side[row],
                taps[row],
            ],
            axis=0,
        )

    odd, near, far = swap_pairs(
        message(slice(0, 2), 0), message(slice(rows - 2, rows), rows - 1), "lat", False
    )
    scale = 1.0 / math.sqrt(total_rows * total_cols)
    cot_lines = cot_t.reshape(rows * cols, chans)
    out_t, term, grad_main, grad_side, taps_all = forward(
        odd.astype(jnp.int32).reshape(1),
        near,
        far,
        field_t.reshape(rows * cols, chans),
        field_side.reshape(rows * 2 * two, chans),
        cot_lines,
        cot_side.reshape(rows * two, chans),
        taps.reshape(rows * 16, chans),
        jnp.transpose(mixing, (1, 2, 0)).reshape(K * chans, chans),
        bias.reshape(1, chans),
        jnp.full((1,), scale, F32),
    )
    share = chans // n_lon
    got = lax.all_to_all(term.reshape(n_lon, share, K * chans), "lon", 0, 0)
    grad_t = backward(
        grad_main,
        grad_side,
        taps_all,
        jnp.transpose(mixing, (1, 0, 2)).reshape(K * chans, chans),
        cot_lines,
    )
    part = jnp.sum(got.astype(F32), axis=0).astype(BF16)
    part, grad_t = lax.optimization_barrier((part, grad_t))
    got = lax.all_to_all(jnp.broadcast_to(part[None], (n_lat, share, K * chans)), "lat", 0, 0)
    grad_mixing = jnp.sum(got.astype(F32), axis=0).reshape(share, K, chans)
    return (
        jnp.transpose(out_t.reshape(rows, cols, chans), (2, 0, 1)),
        jnp.transpose(grad_t.reshape(rows, cols, chans), (2, 0, 1)),
        grad_mixing,
    )


def solution(mesh):
    placed = (
        P(None, "lat", "lon"),
        P(None, "lat", "lon"),
        P(None, "lat", None, None),
        P("lat", None),
        P(),
        P(),
    )
    return jax.shard_map(
        body,
        mesh=mesh,
        in_specs=placed,
        out_specs=(P(None, "lat", "lon"), P(None, "lat", "lon"), P("lon", None, None)),
        check_vma=False,
    )
```
